256 devices in a mesh: seq: 32 (over z_hi, y, core), pair: 8 (over z_lo, x).
Axes of the slice: x: 4, y: 4, z: 8 (z_hi: 4, z_lo: 2; z = z_hi * 2 + z_lo), core: 2. Of those that a mesh axis runs over, the one named last changes fastest.
Arguments:
- student: float32 [20480, 1408], P('seq'), may hold values from -640 to 640
- teacher: float32 [20480, 1408], P('seq'), may hold values from -640 to 640
Outputs:
- student_grad: float32 [20480, 1408], P('seq')
The draws below stay inside these ranges and needn't reach their ends.
All inputs are finite; a program needn't handle non-finite values.
Results may differ from the reference program's by a relative error of at most 0.0059.
Values may be sent and summed in bfloat16 or wider, within the bound.
A program may use at most 64 MiB of HBM per device.

```python
import math
import jax
import jax.numpy as jnp
from jax import lax

D = 1408
TOK_DEV = 640
TOKENS = 20480
N_SEQ = 32


def draw_student(key, part):
    key = jax.random.fold_in(key, 11)
    row_key, col_key, value_key = jax.random.split(key, 3)
    rows = jnp.exp(jax.random.uniform(row_key, (TOKENS, 1), jnp.float32, 0.0, math.log(10.0)))
    values = jnp.clip(jax.random.normal(value_key, (TOKENS, D), jnp.float32), -4.0, 4.0)
    cols = jnp.exp(jax.random.uniform(col_key, (1, D), jnp.float32, 0.0, math.log(10.0)))
    return values * rows * cols


def draw_teacher(key, part):
    key = jax.random.fold_in(key, 23)
    row_key, col_key, value_key = jax.random.split(key, 3)
    rows = jnp.exp(jax.random.uniform(row_key, (TOKENS, 1), jnp.float32, 0.0, math.log(10.0)))
    values = jnp.clip(jax.random.normal(value_key, (TOKENS, D), jnp.float32), -4.0, 4.0)
    cols = jnp.exp(jax.random.uniform(col_key, (1, D), jnp.float32, 0.0, math.log(10.0)))
    return values * rows * cols


def setup_inputs(seed: int = 0) -> dict:
    arg_keys = jax.random.split(jax.random.key(seed), 3)
    student = draw_student(jax.random.fold_in(arg_keys[2], 71), 0)
    teacher = draw_teacher(jax.random.fold_in(arg_keys[2], 71), 0)
    return dict(student=student, teacher=teacher)


def normalize(values, width):
    scale = lax.rsqrt(lax.optimization_barrier(jnp.sum(values * values, axis=1, keepdims=True)) + width * 1e-06)
    return (scale, values * scale)

def relation_block(own_s, own_t, all_s, all_t, margin, weight):
    s_rel = jnp.dot(own_s, all_s.T, preferred_element_type=jnp.float32)
    t_rel = jnp.dot(own_t, all_t.T, preferred_element_type=jnp.float32)
    delta = s_rel - t_rel
    shrink = jnp.maximum(delta - margin, 0.0) + jnp.minimum(delta + margin, 0.0)
    relation = (weight * shrink).astype(jnp.bfloat16)
    return jnp.dot(relation, all_s, preferred_element_type=jnp.float32)

def reference(student, teacher):
    s_scale, s_unit = normalize(student, D)
    t_scale, t_unit = normalize(teacher, D)
    s_half = s_unit.astype(jnp.bfloat16)
    t_half = t_unit.astype(jnp.bfloat16)
    margin = 0.75 / math.sqrt(D)
    weight = 64.0 * D / math.sqrt(TOKENS)
    blocks = (s_half.reshape(N_SEQ, TOK_DEV, D), t_half.reshape(N_SEQ, TOK_DEV, D))

    def one_block(pair_rows):
        return relation_block(pair_rows[0], pair_rows[1], s_half, t_half, margin, weight)
    unit_grad = lax.map(one_block, blocks).reshape(TOKENS, D)
    dotted = lax.optimization_barrier(jnp.sum(s_unit * unit_grad, axis=1, keepdims=True))
    return s_scale * (unit_grad - s_unit * dotted)
```

```python
import functools
import math

import jax
import jax.numpy as jnp
from jax import lax
from jax.experimental import pallas as pl
from jax.experimental.pallas import tpu as pltpu
from jax.sharding import PartitionSpec as P

MESH = pl.DeviceIdType.MESH
UNIT = 80
GROUP = 256
TILE = 320
PARTS = ((0, 512), (512, 512), (1024, 384))
ORDERS = ((0, 1, 2), (1, 2, 0), (2, 0, 1))

NAMES = (
    ["v", "v2", "w"]
    + [item + way for item in ("a", "v", "p", "w") for way in ("+", "-", "f")]
    + ["k0", "k1", "x0", "x1"]
    + [f"r{part}{step}" for part in range(3) for step in range(3)]
    + [f"g{part}{step}" for part in range(3) for step in range(3)]
)
INDEX = {name: i for i, name in enumerate(NAMES)}


def normalize(values, width):
    scale = lax.rsqrt(jnp.sum(values * values, axis=1, keepdims=True) + width * 1e-06)
    return scale, values * scale


def kernel(
    student, teacher, out,
    quarter_s, quarter_t, full_s, full_t, far, cols, own, total, other,
    rs_send, rs_recv, gathered, acc, load_sem, send_sem, recv_sem,
):
    rows, width = student.shape
    margin = 0.75 / math.sqrt(width)
    weight = 64.0 * width / math.sqrt(rows * lax.axis_size("seq"))

    seq, pair = lax.axis_index("seq"), lax.axis_index("pair")
    core, y, z_hi = seq % 2, (seq // 2) % 4, seq // 8
    z_lo, x = pair // 4, pair % 4
    z = z_hi * 2 + z_lo
    side = 2 * z_lo - 1

    def device(x=x, y=y, z=z, core=core):
        return ((z // 2 * 4 + y) * 2 + core, (z % 2) * 4 + x)

    up, down = device(y=(y + 1) % 4), device(y=(y + 3) % 4)
    near_z = device(z=(z + side + 8) % 8)
    after_z, before_z = device(z=(z - 2 * side + 8) % 8), device(z=(z + 2 * side + 8) % 8)
    sibling = device(core=1 - core)
    cube = (device(x=x + 1 - 2 * (x % 2)), device(x=3 - x), device(z=z + 1 - 2 * z_lo))
    bits = (((x + 1) // 2) % 2, x // 2, z_lo)

    def copy(name, src, dst, target):
        i = INDEX[name]
        return pltpu.make_async_remote_copy(
            src_ref=src, dst_ref=dst, send_sem=send_sem.at[i], recv_sem=recv_sem.at[i],
            device_id=target, device_id_type=MESH,
        )

    started = {}

    def send(name, src, dst, target):
        started[name] = copy(name, src, dst, target)
        started[name].start()

    def arrived(*names):
        for name in names:
            started[name].wait_recv()

    first = pl.multiple_of(x * (2 * UNIT), 2 * UNIT)
    loads = [
        pltpu.make_async_copy(student.at[pl.ds(first, 2 * UNIT)], quarter_s, load_sem.at[0]),
        pltpu.make_async_copy(teacher.at[pl.ds(first, 2 * UNIT)], quarter_t, load_sem.at[1]),
        pltpu.make_async_copy(student, full_s, load_sem.at[2]),
        pltpu.make_async_copy(teacher, full_t, load_sem.at[3]),
    ]
    for load in loads:
        load.start()

    barrier = pltpu.get_barrier_semaphore()
    peers = (up, down, near_z, after_z, before_z, sibling) + cube
    for peer in peers:
        pl.semaphore_signal(barrier, inc=1, device_id=peer, device_id_type=MESH)

    def slot(i):
        return cols.at[pl.ds(i * UNIT, UNIT)]

    (A, A_DOWN, A_UP, V, V_DOWN, V_UP, Q, W, A_FAR, V_FAR,
     Q_DOWN, Q_UP, W_DOWN, W_UP, Q_FAR, W_FAR) = range(16)

    loads[0].wait()
    loads[1].wait()
    mine = pl.multiple_of(z_lo * UNIT, UNIT)
    theirs = pl.multiple_of((1 - z_lo) * UNIT, UNIT)
    far[:, :width] = normalize(quarter_s[pl.ds(theirs, UNIT)], width)[1].astype(jnp.bfloat16)
    far[:, width:] = normalize(quarter_t[pl.ds(theirs, UNIT)], width)[1].astype(jnp.bfloat16)
    cols[:UNIT, :width] = normalize(quarter_s[pl.ds(mine, UNIT)], width)[1].astype(jnp.bfloat16)
    cols[:UNIT, width:] = normalize(quarter_t[pl.ds(mine, UNIT)], width)[1].astype(jnp.bfloat16)
    pl.semaphore_wait(barrier, len(peers))
    send("v", far, slot(V), near_z)
    send("a+", slot(A), slot(A_DOWN), up)
    send("a-", slot(A), slot(A_UP), down)
    send("v2", slot(A), slot(Q), near_z)

    loads[2].wait()
    loads[3].wait()
    for half in range(2):

        @pl.loop(0, TILE // UNIT)
        def _(i):
            at = pl.ds(pl.multiple_of(half * TILE + i * UNIT, UNIT), UNIT)
            own[0, at, :width] = normalize(full_s[at], width)[1].astype(jnp.bfloat16)
            own[0, at, width:] = -(normalize(full_t[at], width)[1].astype(jnp.bfloat16))
            total[0, at] = jnp.zeros((UNIT, width), jnp.float32)
            total[1, at] = jnp.zeros((UNIT, width), jnp.float32)

        at = pl.ds(half * TILE, TILE)
        send(f"k{half}", own.at[0, at], own.at[1, at], sibling)

    def relate(group, block, tile):
        at = pl.ds(tile * TILE, TILE)
        tokens = pl.ds(group * GROUP, GROUP)
        delta = lax.dot_general(
            own[block, at, :], cols[tokens, :], (((1,), (1,)), ((), ())),
            preferred_element_type=jnp.float32,
        )
        shrink = jnp.maximum(delta - margin, 0.0) + jnp.minimum(delta + margin, 0.0)
        relation = (weight * shrink).astype(jnp.bfloat16)
        for start, size in PARTS:
            total[block, at, pl.ds(start, size)] += jnp.dot(
                relation, cols[tokens, pl.ds(start, size)], preferred_element_type=jnp.float32
            )

    def relate_all(group):
        @pl.loop(0, 2)
        def _(block):
            for tile in range(rows // TILE):
                relate(group, block, tile)

    arrived("v", "a+", "a-")
    send("v+", slot(V), slot(V_DOWN), up)
    send("v-", slot(V), slot(V_UP), down)
    send("w", slot(V), slot(W), after_z)
    send("af", slot(A_DOWN), slot(A_FAR), up)
    arrived("k0", "k1")
    relate_all(0)
    arrived("v+", "v-", "v2")
    send("vf", slot(V_UP), slot(V_FAR), down)
    send("p+", slot(Q), slot(Q_DOWN), up)
    send("p-", slot(Q), slot(Q_UP), down)
    relate_all(1)
    arrived("w", "af", "vf")
    send("w+", slot(W), slot(W_DOWN), up)
    send("w-", slot(W), slot(W_UP), down)
    relate_all(2)
    arrived("p+", "p-")
    send("pf", slot(Q_DOWN), slot(Q_FAR), up)
    arrived("w+", "w-")
    send("wf", slot(W_UP), slot(W_FAR), down)
    relate_all(3)
    arrived("pf", "wf")
    for tile in range(2):
        at = pl.ds(tile * TILE, TILE)
        relate(4, 1, tile)
        send(f"x{tile}", total.at[1, at], other.at[at], sibling)
    for tile in range(2):
        relate(4, 0, tile)
    arrived("x0", "x1")

    def chunk(order, *place):
        strides = (4, 2, 1)
        index = sum(strides[d] * i for d, i in zip(order, place))
        return pl.ds(pl.multiple_of(index * UNIT, UNIT), UNIT)

    for part, (start, size) in enumerate(PARTS):
        order, at = ORDERS[part], pl.ds(start, size)
        b = [bits[d] for d in order]
        for i in range(4):
            rows_at = chunk(order, 1 - b[0], i // 2, i % 2)
            rs_send[part][i] = (total[0, rows_at, at] + other[rows_at, at]).astype(jnp.bfloat16)
        send(f"r{part}0", rs_send[part].at[0:4], rs_recv[part].at[0:4], cube[order[0]])
    for part, (start, size) in enumerate(PARTS):
        order, at = ORDERS[part], pl.ds(start, size)
        b = [bits[d] for d in order]
        arrived(f"r{part}0")
        for i in range(2):
            rows_at = chunk(order, b[0], 1 - b[1], i)
            got = rs_recv[part][2 * (1 - b[1]) + i].astype(jnp.float32)
            rs_send[part][4 + i] = (
                total[0, rows_at, at] + other[rows_at, at] + got
            ).astype(jnp.bfloat16)
        send(f"r{part}1", rs_send[part].at[4:6], rs_recv[part].at[4:6], cube[order[1]])
    for part, (start, size) in enumerate(PARTS):
        order, at = ORDERS[part], pl.ds(start, size)
        b = [bits[d] for d in order]
        arrived(f"r{part}1")
        for i, place in enumerate((1 - b[2], b[2])):
            rows_at = chunk(order, b[0], b[1], place)
            value = (
                total[0, rows_at, at] + other[rows_at, at]
                + rs_recv[part][2 * b[1] + place].astype(jnp.float32)
                + rs_recv[part][4 + place].astype(jnp.float32)
            )
            if i == 0:
                rs_send[part][6] = value.astype(jnp.bfloat16)
                send(f"r{part}2", rs_send[part].at[6:7], rs_recv[part].at[6:7], cube[order[2]])
            else:
                acc[:, at] = value
    for part, (start, size) in enumerate(PARTS):
        at = pl.ds(start, size)
        arrived(f"r{part}2")
        acc[:, at] += rs_recv[part][6].astype(jnp.float32)

    rows_at = chunk((0, 1, 2), *bits)
    scale, unit = normalize(full_s[rows_at], width)
    unit_grad = acc[...]
    dotted = jnp.sum(unit * unit_grad, axis=1, keepdims=True)
    grad = (scale * (unit_grad - unit * dotted)).astype(jnp.bfloat16)
    for part, (start, size) in enumerate(PARTS):
        order = ORDERS[part]
        b = [bits[d] for d in order]
        gathered[part][b[0], b[1], b[2]] = grad[:, start:start + size]
        mine_at = gathered[part].at[b[0], b[1], b[2]]
        send(f"g{part}0", mine_at, mine_at, cube[order[2]])
    for part in range(3):
        order = ORDERS[part]
        b = [bits[d] for d in order]
        arrived(f"g{part}0")
        mine_at = gathered[part].at[b[0], b[1]]
        send(f"g{part}1", mine_at, mine_at, cube[order[1]])
    for part in range(3):
        order = ORDERS[part]
        b = [bits[d] for d in order]
        arrived(f"g{part}1")
        mine_at = gathered[part].at[b[0]]
        send(f"g{part}2", mine_at, mine_at, cube[order[0]])
    for part, (start, size) in enumerate(PARTS):
        order = ORDERS[part]
        arrived(f"g{part}2")
        for i in range(8):
            place = (i // 4, i // 2 % 2, i % 2)
            out[i * UNIT:(i + 1) * UNIT, start:start + size] = gathered[part][
                tuple(place[d] for d in order)
            ]
    for name in NAMES:
        started[name].wait_send()


def local(student, teacher):
    rows, width = student.shape
    bf16, f32 = jnp.bfloat16, jnp.float32

    def body(student, teacher, out, *scratch):
        plain, parts = scratch[:9], scratch[9:18]
        kernel(student, teacher, out, *plain, parts[0:3], parts[3:6], parts[6:9], *scratch[18:])

    grad = pl.pallas_call(
        body,
        out_shape=jax.ShapeDtypeStruct((rows, width), bf16),
        in_specs=[pl.BlockSpec(memory_space=pl.ANY)] * 2,
        out_specs=pl.BlockSpec(memory_space=pltpu.VMEM),
        scratch_shapes=[
            pltpu.VMEM((2 * UNIT, width), f32),
            pltpu.VMEM((2 * UNIT, width), f32),
            pltpu.VMEM((rows, width), f32),
            pltpu.VMEM((rows, width), f32),
            pltpu.VMEM((UNIT, 2 * width), bf16),
            pltpu.VMEM((2 * rows, 2 * width), bf16),
            pltpu.VMEM((2, rows, 2 * width), bf16),
            pltpu.VMEM((2, rows, width), f32),
            pltpu.VMEM((rows, width), f32),
        ]
        + [pltpu.VMEM((7, UNIT, size), bf16) for _, size in PARTS] * 2
        + [pltpu.VMEM((2, 2, 2, UNIT, size), bf16) for _, size in PARTS]
        + [
            pltpu.VMEM((UNIT, width), f32),
            pltpu.SemaphoreType.DMA((4,)),
            pltpu.SemaphoreType.DMA((len(NAMES),)),
            pltpu.SemaphoreType.DMA((len(NAMES),)),
        ],
        compiler_params=pltpu.CompilerParams(
            collective_id=0, has_side_effects=True, vmem_limit_bytes=56 << 20
        ),
        name="relation_grad",
    )(student, teacher)
    return grad.astype(f32)


def solution(mesh):
    placed = (P("seq", None), P("seq", None))
    return jax.shard_map(
        local, mesh=mesh, in_specs=placed, out_specs=P("seq", None), check_vma=False
    )
```

```python
import functools
import math

import jax
import jax.numpy as jnp
from jax import lax
from jax.experimental import pallas as pl
from jax.experimental.pallas import tpu as pltpu
from jax.sharding import PartitionSpec as P

MESH = pl.DeviceIdType.MESH
UNIT = 80
GROUP = 256
TILE = 320
WAVES = ((0, 48), (48, 32))
PARTS = ((0, 512), (512, 512), (1024, 384))
ORDERS = ((0, 1, 2), (1, 2, 0), (2, 0, 1))

NAMES = (
    ["v", "q", "w", "qd", "qu", "qf"]
    + [item + way for item in ("a", "v", "w") for way in ("+", "-", "f")]
    + ["k0", "k1", "x", "e0", "e1", "e2", "e3"]
    + [f"{kind}{part}{step}{wave}" for kind in "rg"
       for part in range(3) for step in range(3) for wave in range(2)]
)
INDEX = {name: i for i, name in enumerate(NAMES)}


def normalize(values, width):
    scale = lax.rsqrt(jnp.sum(values * values, axis=1, keepdims=True) + width * 1e-06)
    return scale, values * scale


def kernel(
    student, teacher, out,
    quarter_s, quarter_t, full_s, full_t, far, cols, extra, own, total, other,
    rs_send, rs_recv, gathered, acc, load_sem, send_sem, recv_sem,
):
    rows, width = student.shape
    margin = 0.75 / math.sqrt(width)
    weight = 64.0 * width / math.sqrt(rows * lax.axis_size("seq"))

    seq, pair = lax.axis_index("seq"), lax.axis_index("pair")
    core, y, z_hi = seq % 2, (seq // 2) % 4, seq // 8
    z_lo, x = pair // 4, pair % 4
    z = z_hi * 2 + z_lo
    side = 2 * z_lo - 1

    def device(x=x, y=y, z=z, core=core):
        return ((z // 2 * 4 + y) * 2 + core, (z % 2) * 4 + x)

    up, down = device(y=(y + 1) % 4), device(y=(y + 3) % 4)
    near_z = device(z=(z + side + 8) % 8)
    after_z, before_z = device(z=(z - 2 * side + 8) % 8), device(z=(z + 2 * side + 8) % 8)
    sibling = device(core=1 - core)
    cube = (device(x=x + 1 - 2 * (x % 2)), device(x=3 - x), device(z=z + 1 - 2 * z_lo))
    bits = (((x + 1) // 2) % 2, x // 2, z_lo)

    def copy(name, src, dst, target):
        i = INDEX[name]
        return pltpu.make_async_remote_copy(
            src_ref=src, dst_ref=dst, send_sem=send_sem.at[i], recv_sem=recv_sem.at[i],
            device_id=target, device_id_type=MESH,
        )

    started = {}

    def send(name, src, dst, target):
        started[name] = copy(name, src, dst, target)
        started[name].start()

    def arrived(*names):
        for name in names:
            started[name].wait_recv()

    first = pl.multiple_of(x * (2 * UNIT), 2 * UNIT)
    loads = [
        pltpu.make_async_copy(student.at[pl.ds(first, 2 * UNIT)], quarter_s, load_sem.at[0]),
        pltpu.make_async_copy(teacher.at[pl.ds(first, 2 * UNIT)], quarter_t, load_sem.at[1]),
        pltpu.make_async_copy(student, full_s, load_sem.at[2]),
        pltpu.make_async_copy(teacher, full_t, load_sem.at[3]),
    ]
    for load in loads:
        load.start()

    barrier = pltpu.get_barrier_semaphore()
    peers = (up, down, near_z, after_z, before_z, sibling) + cube
    for peer in peers:
        pl.semaphore_signal(barrier, inc=1, device_id=peer, device_id_type=MESH)

    def slot(i):
        return cols.at[pl.ds(i * UNIT, UNIT)]

    (A, A_DOWN, A_UP, V, V_DOWN, V_UP, W, A_FAR, V_FAR, Q_DOWN,
     W_DOWN, W_UP, Q_UP, Q_FAR, W_FAR, Q) = range(16)

    loads[0].wait()
    loads[1].wait()
    mine = pl.multiple_of(z_lo * UNIT, UNIT)
    theirs = pl.multiple_of((1 - z_lo) * UNIT, UNIT)
    far[:, :width] = normalize(quarter_s[pl.ds(theirs, UNIT)], width)[1].astype(jnp.bfloat16)
    far[:, width:] = normalize(quarter_t[pl.ds(theirs, UNIT)], width)[1].astype(jnp.bfloat16)
    cols[:UNIT, :width] = normalize(quarter_s[pl.ds(mine, UNIT)], width)[1].astype(jnp.bfloat16)
    cols[:UNIT, width:] = normalize(quarter_t[pl.ds(mine, UNIT)], width)[1].astype(jnp.bfloat16)
    pl.semaphore_wait(barrier, len(peers))
    send("v", far, slot(V), near_z)
    send("a+", slot(A), slot(A_DOWN), up)
    send("a-", slot(A), slot(A_UP), down)

    loads[2].wait()
    loads[3].wait()
    for half in range(2):

        @pl.loop(0, TILE // UNIT)
        def _(i):
            at = pl.ds(pl.multiple_of(half * TILE + i * UNIT, UNIT), UNIT)
            own[0, at, :width] = normalize(full_s[at], width)[1].astype(jnp.bfloat16)
            own[0, at, width:] = -(normalize(full_t[at], width)[1].astype(jnp.bfloat16))
            total[0, at] = jnp.zeros((UNIT, width), jnp.float32)
            total[1, at] = jnp.zeros((UNIT, width), jnp.float32)

        at = pl.ds(half * TILE, TILE)
        send(f"k{half}", own.at[0, at], own.at[1, at], sibling)

    def relate(partner, start, block, tile):
        at, tokens = pl.ds(tile * TILE, TILE), pl.ds(start, GROUP)
        delta = lax.dot_general(
            own[block, at, :], partner[tokens, :], (((1,), (1,)), ((), ())),
            preferred_element_type=jnp.float32,
        )
        shrink = jnp.maximum(delta - margin, 0.0) + jnp.minimum(delta + margin, 0.0)
        relation = (weight * shrink).astype(jnp.bfloat16)
        for first, size in PARTS:
            total[block, at, pl.ds(first, size)] += jnp.dot(
                relation, partner[tokens, pl.ds(first, size)], preferred_element_type=jnp.float32
            )

    def relate_all(group):
        @pl.loop(0, 2)
        def _(block):
            for tile in range(rows // TILE):
                relate(cols, group * GROUP, block, tile)

    def relate_own(partner, start):
        for tile in range(rows // TILE):
            relate(partner, start, 0, tile)

    def share(name, start, size):
        send(name, cols.at[pl.ds(4 * GROUP + start, size)], extra.at[pl.ds(start, size)], sibling)

    arrived("v")
    send("v+", slot(V), slot(V_DOWN), up)
    send("v-", slot(V), slot(V_UP), down)
    send("w", slot(V), slot(W), after_z)
    arrived("a+", "a-")
    send("af", slot(A_DOWN), slot(A_FAR), up)
    send("qd", slot(A_DOWN), slot(Q_DOWN), near_z)
    send("qu", slot(A_UP), slot(Q_UP), near_z)
    send("q", slot(A), slot(Q), near_z)
    arrived("k0", "k1")
    relate_all(0)
    arrived("v+", "v-")
    send("vf", slot(V_UP), slot(V_FAR), down)
    arrived("w")
    send("w+", slot(W), slot(W_DOWN), up)
    send("w-", slot(W), slot(W_UP), down)
    relate_all(1)
    arrived("qd")
    send("qf", slot(Q_DOWN), slot(Q_FAR), up)
    arrived("af", "vf")
    relate_all(2)
    arrived("w-")
    send("wf", slot(W_UP), slot(W_FAR), down)
    arrived("w+", "qu")
    share("e0", 0, 16)
    relate_all(3)
    send("x", total.at[1], other, sibling)
    for i, name in enumerate(("qf", "wf", "q")):
        arrived(name)
        share(f"e{i + 1}", 16 + i * UNIT, UNIT)
    relate_own(cols, 4 * GROUP)
    arrived("x", "e0", "e1", "e2", "e3")
    relate_own(extra, 0)

    def chunk(wave, order, *place):
        strides = (4, 2, 1)
        index = sum(strides[d] * i for d, i in zip(order, place))
        skip, size = WAVES[wave]
        return pl.ds(pl.multiple_of(index * UNIT + skip, 16), size)

    def each():
        for wave in range(2):
            for part, (start, size) in enumerate(PARTS):
                order = ORDERS[part]
                yield wave, part, order, [bits[d] for d in order], pl.ds(start, size), pl.ds(*WAVES[wave])

    def reduce(step, wave, part, order, first, count):
        at = (pl.ds(first, count), pl.ds(*WAVES[wave]))
        send(f"r{part}{step}{wave}", rs_send[part].at[at], rs_recv[part].at[at], cube[order[step]])

    for wave, part, order, b, at, sub in each():
        for i in range(4):
            rows_at = chunk(wave, order, 1 - b[0], i // 2, i % 2)
            rs_send[part][i, sub] = (total[0, rows_at, at] + other[rows_at, at]).astype(jnp.bfloat16)
        reduce(0, wave, part, order, 0, 4)
    for wave, part, order, b, at, sub in each():
        arrived(f"r{part}0{wave}")
        for i in range(2):
            rows_at = chunk(wave, order, b[0], 1 - b[1], i)
            got = rs_recv[part][2 * (1 - b[1]) + i, sub].astype(jnp.float32)
            rs_send[part][4 + i, sub] = (
                total[0, rows_at, at] + other[rows_at, at] + got
            ).astype(jnp.bfloat16)
        reduce(1, wave, part, order, 4, 2)
    for wave, part, order, b, at, sub in each():
        arrived(f"r{part}1{wave}")
        for i, place in enumerate((1 - b[2], b[2])):
            rows_at = chunk(wave, order, b[0], b[1], place)
            value = (
                total[0, rows_at, at] + other[rows_at, at]
                + rs_recv[part][2 * b[1] + place, sub].astype(jnp.float32)
                + rs_recv[part][4 + place, sub].astype(jnp.float32)
            )
            if i == 0:
                rs_send[part][6, sub] = value.astype(jnp.bfloat16)
                reduce(2, wave, part, order, 6, 1)
            else:
                acc[sub, at] = value

    def spread(step, wave, part, order, *place):
        there = gathered[part].at[place + (slice(None),) * step + (pl.ds(*WAVES[wave]),)]
        send(f"g{part}{step}{wave}", there, there, cube[order[2 - step]])

    for wave in range(2):
        sub = pl.ds(*WAVES[wave])
        for part, (start, size) in enumerate(PARTS):
            arrived(f"r{part}2{wave}")
            acc[sub, start:start + size] += rs_recv[part][6, sub].astype(jnp.float32)
        scale, unit = normalize(full_s[chunk(wave, (0, 1, 2), *bits)], width)
        unit_grad = acc[sub]
        dotted = jnp.sum(unit * unit_grad, axis=1, keepdims=True)
        grad = (scale * (unit_grad - unit * dotted)).astype(jnp.bfloat16)
        for part, (start, size) in enumerate(PARTS):
            order = ORDERS[part]
            b = [bits[d] for d in order]
            gathered[part][b[0], b[1], b[2], sub] = grad[:, start:start + size]
            spread(0, wave, part, order, *b)
    for wave, part, order, b, at, sub in each():
        arrived(f"g{part}0{wave}")
        spread(1, wave, part, order, b[0], b[1])
    for wave, part, order, b, at, sub in each():
        arrived(f"g{part}1{wave}")
        spread(2, wave, part, order, b[0])
    for wave, part, order, b, at, sub in each():
        arrived(f"g{part}2{wave}")
        for i in range(8):
            place = (i // 4, i // 2 % 2, i % 2)
            out[chunk(wave, (0, 1, 2), *place), at] = gathered[part][
                tuple(place[d] for d in order) + (sub,)
            ]
    for name in NAMES:
        started[name].wait_send()


def local(student, teacher):
    rows, width = student.shape
    bf16, f32 = jnp.bfloat16, jnp.float32

    def body(student, teacher, out, *scratch):
        plain, parts = scratch[:10], scratch[10:19]
        kernel(student, teacher, out, *plain, parts[0:3], parts[3:6], parts[6:9], *scratch[19:])

    grad = pl.pallas_call(
        body,
        out_shape=jax.ShapeDtypeStruct((rows, width), bf16),
        in_specs=[pl.BlockSpec(memory_space=pl.ANY)] * 2,
        out_specs=pl.BlockSpec(memory_space=pltpu.VMEM),
        scratch_shapes=[
            pltpu.VMEM((2 * UNIT, width), f32),
            pltpu.VMEM((2 * UNIT, width), f32),
            pltpu.VMEM((rows, width), f32),
            pltpu.VMEM((rows, width), f32),
            pltpu.VMEM((UNIT, 2 * width), bf16),
            pltpu.VMEM((2 * rows, 2 * width), bf16),
            pltpu.VMEM((GROUP, 2 * width), bf16),
            pltpu.VMEM((2, rows, 2 * width), bf16),
            pltpu.VMEM((2, rows, width), f32),
            pltpu.VMEM((rows, width), f32),
        ]
        + [pltpu.VMEM((7, UNIT, size), bf16) for _, size in PARTS] * 2
        + [pltpu.VMEM((2, 2, 2, UNIT, size), bf16) for _, size in PARTS]
        + [
            pltpu.VMEM((UNIT, width), f32),
            pltpu.SemaphoreType.DMA((4,)),
            pltpu.SemaphoreType.DMA((len(NAMES),)),
            pltpu.SemaphoreType.DMA((len(NAMES),)),
        ],
        compiler_params=pltpu.CompilerParams(
            collective_id=0, has_side_effects=True, vmem_limit_bytes=56 << 20
        ),
        name="relation_grad",
    )(student, teacher)
    return grad.astype(f32)


def solution(mesh):
    placed = (P("seq", None), P("seq", None))
    return jax.shard_map(
        local, mesh=mesh, in_specs=placed, out_specs=P("seq", None), check_vma=False
    )
```

```python
import functools
import math

import jax
import jax.numpy as jnp
from jax import lax
from jax.experimental import pallas as pl
from jax.experimental.pallas import tpu as pltpu
from jax.sharding import PartitionSpec as P

MESH = pl.DeviceIdType.MESH
UNIT = 80
GROUP = 256
TILE = 320
HALVES = ((0, 48), (48, 32))
WAVES = ((0, 32), (32, 32), (64, 16))
APART = 2
PARTS = ((0, 512), (512, 512), (1024, 384))
ORDERS = ((0, 1, 2), (1, 2, 0), (2, 0, 1))

NAMES = (
    [f"{item}{half}" for half in range(2) for item in (
        "v", "q", "w", "qd", "qu", "qf", "a+", "a-", "af", "v+", "v-", "vf", "w+", "w-", "wf",
        "eqf", "ewf", "eq", "k", "x")]
    + ["e"]
    + [f"{kind}{part}{step}{wave}" for kind in "rg"
       for part in range(3) for step in range(3) for wave in range(len(WAVES))]
)
INDEX = {name: i for i, name in enumerate(NAMES)}


def normalize(values, width):
    scale = lax.rsqrt(jnp.sum(values * values, axis=1, keepdims=True) + width * 1e-06)
    return scale, values * scale


def kernel(
    student, teacher, out,
    quarter_s, quarter_t, full_s, full_t, far, cols, extra, own, total, other,
    rs_send, rs_recv, gathered, acc, load_sem, send_sem, recv_sem,
):
    rows, width = student.shape
    margin = 0.75 / math.sqrt(width)
    weight = 64.0 * width / math.sqrt(rows * lax.axis_size("seq"))

    seq, pair = lax.axis_index("seq"), lax.axis_index("pair")
    core, y, z_hi = seq % 2, (seq // 2) % 4, seq // 8
    z_lo, x = pair // 4, pair % 4
    z = z_hi * 2 + z_lo
    side = 2 * z_lo - 1

    def device(x=x, y=y, z=z, core=core):
        return ((z // 2 * 4 + y) * 2 + core, (z % 2) * 4 + x)

    up, down = device(y=(y + 1) % 4), device(y=(y + 3) % 4)
    near_z = device(z=(z + side + 8) % 8)
    after_z, before_z = device(z=(z - 2 * side + 8) % 8), device(z=(z + 2 * side + 8) % 8)
    sibling = device(core=1 - core)
    cube = (device(x=x + 1 - 2 * (x % 2)), device(x=3 - x), device(z=z + 1 - 2 * z_lo))
    bits = (((x + 1) // 2) % 2, x // 2, z_lo)

    def copy(name, src, dst, target):
        i = INDEX[name]
        return pltpu.make_async_remote_copy(
            src_ref=src, dst_ref=dst, send_sem=send_sem.at[i], recv_sem=recv_sem.at[i],
            device_id=target, device_id_type=MESH,
        )

    started = {}

    def send(name, src, dst, target):
        started[name] = copy(name, src, dst, target)
        started[name].start()

    def arrived(*names):
        for name in names:
            started[name].wait_recv()

    barrier = pltpu.get_barrier_semaphore()
    peers = (up, down, near_z, after_z, before_z, sibling) + cube
    for peer in peers:
        pl.semaphore_signal(barrier, inc=1, device_id=peer, device_id_type=MESH)

    first = pl.multiple_of(x * (2 * UNIT), 2 * UNIT)
    loads = [
        pltpu.make_async_copy(student.at[pl.ds(first, 2 * UNIT)], quarter_s, load_sem.at[0]),
        pltpu.make_async_copy(teacher.at[pl.ds(first, 2 * UNIT)], quarter_t, load_sem.at[1]),
        pltpu.make_async_copy(student, full_s, load_sem.at[2]),
        pltpu.make_async_copy(teacher, full_t, load_sem.at[3]),
    ]
    loads[0].start()
    loads[1].start()

    (A, A_DOWN, A_UP, V, V_DOWN, V_UP, W, A_FAR, V_FAR, Q_DOWN,
     W_DOWN, W_UP, Q_UP, Q_FAR, W_FAR, Q) = range(16)

    def move(name, half, src, dst, target):
        skip, size = HALVES[half]
        send(f"{name}{half}", cols.at[pl.ds(src * UNIT + skip, size)],
             cols.at[pl.ds(dst * UNIT + skip, size)], target)

    loads[0].wait()
    loads[1].wait()
    loads[2].start()
    loads[3].start()
    for half, (skip, size) in enumerate(HALVES):
        here, mine, theirs = (
            pl.ds(pl.multiple_of(at + skip, 16), size) for at in (0, z_lo * UNIT, (1 - z_lo) * UNIT)
        )
        far[here, :width] = normalize(quarter_s[theirs], width)[1].astype(jnp.bfloat16)
        far[here, width:] = normalize(quarter_t[theirs], width)[1].astype(jnp.bfloat16)
        cols[here, :width] = normalize(quarter_s[mine], width)[1].astype(jnp.bfloat16)
        cols[here, width:] = normalize(quarter_t[mine], width)[1].astype(jnp.bfloat16)
        if half == 0:
            pl.semaphore_wait(barrier, len(peers))
        send(f"v{half}", far.at[here], cols.at[pl.ds(V * UNIT + skip, size)], near_z)
        move("a+", half, A, A_DOWN, up)
        move("a-", half, A, A_UP, down)

    loads[2].wait()
    loads[3].wait()
    for half in range(2):

        @pl.loop(0, TILE // UNIT)
        def _(i):
            at = pl.ds(pl.multiple_of(half * TILE + i * UNIT, UNIT), UNIT)
            own[0, at, :width] = normalize(full_s[at], width)[1].astype(jnp.bfloat16)
            own[0, at, width:] = -(normalize(full_t[at], width)[1].astype(jnp.bfloat16))
            total[0, at] = jnp.zeros((UNIT, width), jnp.float32)
            total[1, at] = jnp.zeros((UNIT, width), jnp.float32)

        at = pl.ds(half * TILE, TILE)
        send(f"k{half}", own.at[0, at], own.at[1, at], sibling)

    def relate(partner, start, block, tile):
        at, tokens = pl.ds(tile * TILE, TILE), pl.ds(start, GROUP)
        delta = lax.dot_general(
            own[block, at, :], partner[tokens, :], (((1,), (1,)), ((), ())),
            preferred_element_type=jnp.float32,
        )
        shrink = jnp.maximum(delta - margin, 0.0) + jnp.minimum(delta + margin, 0.0)
        relation = (weight * shrink).astype(jnp.bfloat16)
        for first, size in PARTS:
            total[block, at, pl.ds(first, size)] += jnp.dot(
                relation, partner[tokens, pl.ds(first, size)], preferred_element_type=jnp.float32
            )

    def relate_all(group):
        @pl.loop(0, 2)
        def _(block):
            for tile in range(rows // TILE):
                relate(cols, group * GROUP, block, tile)

    def relate_own(partner, start):
        for tile in range(rows // TILE):
            relate(partner, start, 0, tile)

    def share(name, start, size):
        send(name, cols.at[pl.ds(4 * GROUP + start, size)], extra.at[pl.ds(start, size)], sibling)

    for half in range(2):
        arrived(f"v{half}")
        move("v+", half, V, V_DOWN, up)
        move("v-", half, V, V_UP, down)
        move("w", half, V, W, after_z)
    for half in range(2):
        arrived(f"a+{half}", f"a-{half}")
        move("qd", half, A_DOWN, Q_DOWN, near_z)
        move("af", half, A_DOWN, A_FAR, up)
    for half in range(2):
        move("qu", half, A_UP, Q_UP, near_z)
    for half in range(2):
        move("q", half, A, Q, near_z)
    arrived("k0", "k1")
    relate_all(0)
    for half in range(2):
        arrived(f"v+{half}", f"v-{half}")
        move("vf", half, V_UP, V_FAR, down)
    for half in range(2):
        arrived(f"w{half}")
        move("w+", half, W, W_DOWN, up)
        move("w-", half, W, W_UP, down)
    relate_all(1)
    for half in range(2):
        arrived(f"qd{half}")
        move("qf", half, Q_DOWN, Q_FAR, up)
    arrived("af0", "vf0", "af1", "vf1")
    relate_all(2)
    for half in range(2):
        arrived(f"w-{half}", f"w+{half}")
        move("wf", half, W_UP, W_FAR, down)
    arrived("qu0", "qu1")
    share("e", 0, 16)
    for tile in range(2):
        at = pl.ds(tile * TILE, TILE)
        relate(cols, 3 * GROUP, 1, tile)
        send(f"x{tile}", total.at[1, at], other.at[at], sibling)
    relate_own(cols, 3 * GROUP)
    for half, (skip, size) in enumerate(HALVES):
        for i, name in enumerate(("qf", "wf", "q")):
            arrived(f"{name}{half}")
            share(f"e{name}{half}", 16 + i * UNIT + skip, size)
    relate_own(cols, 4 * GROUP)
    arrived("x0", "x1", "e", "eqf0", "ewf0", "eq0", "eqf1", "ewf1", "eq1")
    relate_own(extra, 0)

    def chunk(wave, order, *place):
        strides = (4, 2, 1)
        index = sum(strides[d] * i for d, i in zip(order, place))
        skip, size = WAVES[wave]
        return pl.ds(pl.multiple_of(index * UNIT + skip, 16), size)

    def parts(wave):
        for part, (start, size) in enumerate(PARTS):
            order = ORDERS[(part + wave) % 3]
            yield part, order, [bits[d] for d in order], pl.ds(start, size)

    def reduce(step, wave, part, order, first, count):
        at = (pl.ds(first, count), pl.ds(*WAVES[wave]))
        send(f"r{part}{step}{wave}", rs_send[part].at[at], rs_recv[part].at[at], cube[order[step]])

    def spread(step, wave, part, order, *place):
        there = gathered[part].at[place + (slice(None),) * step + (pl.ds(*WAVES[wave]),)]
        send(f"g{part}{step}{wave}", there, there, cube[order[2 - step]])

    def halve_first(wave):
        sub = pl.ds(*WAVES[wave])
        for part, order, b, at in parts(wave):
            for i in range(4):
                rows_at = chunk(wave, order, 1 - b[0], i // 2, i % 2)
                rs_send[part][i, sub] = (total[0, rows_at, at] + other[rows_at, at]).astype(jnp.bfloat16)
            reduce(0, wave, part, order, 0, 4)

    def halve_second(wave):
        sub = pl.ds(*WAVES[wave])
        for part, order, b, at in parts(wave):
            arrived(f"r{part}0{wave}")
            for i in range(2):
                rows_at = chunk(wave, order, b[0], 1 - b[1], i)
                got = rs_recv[part][2 * (1 - b[1]) + i, sub].astype(jnp.float32)
                rs_send[part][4 + i, sub] = (
                    total[0, rows_at, at] + other[rows_at, at] + got
                ).astype(jnp.bfloat16)
            reduce(1, wave, part, order, 4, 2)

    def halve_third(wave):
        sub = pl.ds(*WAVES[wave])
        for part, order, b, at in parts(wave):
            arrived(f"r{part}1{wave}")
            for i, place in enumerate((1 - b[2], b[2])):
                rows_at = chunk(wave, order, b[0], b[1], place)
                value = (
                    total[0, rows_at, at] + other[rows_at, at]
                    + rs_recv[part][2 * b[1] + place, sub].astype(jnp.float32)
                    + rs_recv[part][4 + place, sub].astype(jnp.float32)
                )
                if i == 0:
                    rs_send[part][6, sub] = value.astype(jnp.bfloat16)
                    reduce(2, wave, part, order, 6, 1)
                else:
                    acc[sub, at] = value

    def finish(wave):
        sub = pl.ds(*WAVES[wave])
        for part, order, b, at in parts(wave):
            arrived(f"r{part}2{wave}")
            acc[sub, at] += rs_recv[part][6, sub].astype(jnp.float32)
        scale, unit = normalize(full_s[chunk(wave, (0, 1, 2), *bits)], width)
        unit_grad = acc[sub]
        dotted = jnp.sum(unit * unit_grad, axis=1, keepdims=True)
        grad = (scale * (unit_grad - unit * dotted)).astype(jnp.bfloat16)
        for part, order, b, at in parts(wave):
            start, size = PARTS[part]
            gathered[part][b[0], b[1], b[2], sub] = grad[:, start:start + size]
            spread(0, wave, part, order, *b)

    def double_second(wave):
        for part, order, b, at in parts(wave):
            arrived(f"g{part}0{wave}")
            spread(1, wave, part, order, b[0], b[1])

    def double_third(wave):
        for part, order, b, at in parts(wave):
            arrived(f"g{part}1{wave}")
            spread(2, wave, part, order, b[0])

    def emit(wave):
        sub = pl.ds(*WAVES[wave])
        for part, order, b, at in parts(wave):
            arrived(f"g{part}2{wave}")
            for i in range(8):
                place = (i // 4, i // 2 % 2, i % 2)
                out[chunk(wave, (0, 1, 2), *place), at] = gathered[part][
                    tuple(place[d] for d in order) + (sub,)
                ]

    stages = (halve_first, halve_second, halve_third, finish, double_second, double_third, emit)
    steps = [(wave + APART * i, i, wave) for i in range(len(stages)) for wave in range(len(WAVES))]
    for _, i, wave in sorted(steps):
        stages[i](wave)
    for name in NAMES:
        started[name].wait_send()


def local(student, teacher):
    rows, width = student.shape
    bf16, f32 = jnp.bfloat16, jnp.float32

    def body(student, teacher, out, *scratch):
        plain, parts = scratch[:10], scratch[10:19]
        kernel(student, teacher, out, *plain, parts[0:3], parts[3:6], parts[6:9], *scratch[19:])

    grad = pl.pallas_call(
        body,
        out_shape=pltpu.VMEM((rows, width), bf16),
        in_specs=[pl.BlockSpec(memory_space=pl.ANY)] * 2,
        out_specs=pl.BlockSpec(memory_space=pltpu.VMEM),
        scratch_shapes=[
            pltpu.VMEM((2 * UNIT, width), f32),
            pltpu.VMEM((2 * UNIT, width), f32),
            pltpu.VMEM((rows, width), f32),
            pltpu.VMEM((rows, width), f32),
            pltpu.VMEM((UNIT, 2 * width), bf16),
            pltpu.VMEM((2 * rows, 2 * width), bf16),
            pltpu.VMEM((GROUP, 2 * width), bf16),
            pltpu.VMEM((2, rows, 2 * width), bf16),
            pltpu.VMEM((2, rows, width), f32),
            pltpu.VMEM((rows, width), f32),
        ]
        + [pltpu.VMEM((7, UNIT, size), bf16) for _, size in PARTS] * 2
        + [pltpu.VMEM((2, 2, 2, UNIT, size), bf16) for _, size in PARTS]
        + [
            pltpu.VMEM((UNIT, width), f32),
            pltpu.SemaphoreType.DMA((4,)),
            pltpu.SemaphoreType.DMA((len(NAMES),)),
            pltpu.SemaphoreType.DMA((len(NAMES),)),
        ],
        compiler_params=pltpu.CompilerParams(
            collective_id=0, has_side_effects=True, vmem_limit_bytes=56 << 20
        ),
        name="relation_grad",
    )(student, teacher)
    return grad.astype(f32)


def solution(mesh):
    placed = (P("seq", None), P("seq", None))
    return jax.shard_map(
        local, mesh=mesh, in_specs=placed, out_specs=P("seq", None), check_vma=False
    )
```

```python
import functools
import math

import jax
import jax.numpy as jnp
from jax import lax
from jax.experimental import pallas as pl
from jax.experimental.pallas import tpu as pltpu
from jax.sharding import PartitionSpec as P

MESH = pl.DeviceIdType.MESH
UNIT = 80
GROUP = 256
TILE = 320
WAVES = ((0, 32), (32, 32), (64, 16))
APART = 2
PARTS = ((0, 512), (512, 512), (1024, 384))
ORDERS = ((0, 1, 2), (1, 2, 0), (2, 0, 1))

NAMES = (
    ["v", "q", "w", "qd", "qu", "qf", "a+", "a-", "af", "v+", "v-", "vf", "w+", "w-", "wf"]
    + ["e", "eqf", "ewf", "eq", "k0", "k1", "x0", "x1"]
    + [f"{kind}{part}{step}{wave}" for kind in "rg"
       for part in range(3) for step in range(3) for wave in range(len(WAVES))]
)
INDEX = {name: i for i, name in enumerate(NAMES)}


def normalize(values, width):
    scale = lax.rsqrt(jnp.sum(values * values, axis=1, keepdims=True) + width * 1e-06)
    return scale, values * scale


def kernel(
    student, teacher, out,
    quarter_s, quarter_t, full_s, full_t, far, cols, extra, own, total, other,
    rs_send, rs_recv, gathered, acc, own_unit, own_scale, load_sem, send_sem, recv_sem,
):
    rows, width = student.shape
    margin = 0.75 / math.sqrt(width)
    weight = 64.0 * width / math.sqrt(rows * lax.axis_size("seq"))

    seq, pair = lax.axis_index("seq"), lax.axis_index("pair")
    core, y, z_hi = seq % 2, (seq // 2) % 4, seq // 8
    z_lo, x = pair // 4, pair % 4
    z = z_hi * 2 + z_lo
    side = 2 * z_lo - 1

    def device(x=x, y=y, z=z, core=core):
        return ((z // 2 * 4 + y) * 2 + core, (z % 2) * 4 + x)

    up, down = device(y=(y + 1) % 4), device(y=(y + 3) % 4)
    near_z = device(z=(z + side + 8) % 8)
    after_z, before_z = device(z=(z - 2 * side + 8) % 8), device(z=(z + 2 * side + 8) % 8)
    sibling = device(core=1 - core)
    cube = (device(x=x + 1 - 2 * (x % 2)), device(x=3 - x), device(z=z + 1 - 2 * z_lo))
    bits = (((x + 1) // 2) % 2, x // 2, z_lo)

    def copy(name, src, dst, target):
        i = INDEX[name]
        return pltpu.make_async_remote_copy(
            src_ref=src, dst_ref=dst, send_sem=send_sem.at[i], recv_sem=recv_sem.at[i],
            device_id=target, device_id_type=MESH,
        )

    started = {}

    def send(name, src, dst, target):
        started[name] = copy(name, src, dst, target)
        started[name].start()

    def arrived(*names):
        for name in names:
            started[name].wait_recv()

    barrier = pltpu.get_barrier_semaphore()
    peers = (up, down, near_z, after_z, before_z, sibling) + cube
    for peer in peers:
        pl.semaphore_signal(barrier, inc=1, device_id=peer, device_id_type=MESH)

    first = pl.multiple_of(x * (2 * UNIT), 2 * UNIT)
    loads = [
        pltpu.make_async_copy(student.at[pl.ds(first, 2 * UNIT)], quarter_s, load_sem.at[0]),
        pltpu.make_async_copy(teacher.at[pl.ds(first, 2 * UNIT)], quarter_t, load_sem.at[1]),
        pltpu.make_async_copy(student, full_s, load_sem.at[2]),
        pltpu.make_async_copy(teacher, full_t, load_sem.at[3]),
    ]
    loads[0].start()
    loads[1].start()

    (A, A_DOWN, A_UP, V, V_DOWN, V_UP, W, A_FAR, V_FAR, Q_DOWN,
     W_DOWN, W_UP, Q_UP, Q_FAR, W_FAR, Q) = range(16)

    loads[0].wait()
    loads[1].wait()
    loads[2].start()
    loads[3].start()
    def quarter(dst, start):
        at = pl.ds(pl.multiple_of(start * UNIT, UNIT), UNIT)
        dst[:, :width] = normalize(quarter_s[at], width)[1].astype(jnp.bfloat16)
        dst[:, width:] = normalize(quarter_t[at], width)[1].astype(jnp.bfloat16)

    def slot(i):
        return cols.at[pl.ds(i * UNIT, UNIT)]

    def move(name, src, dst, target):
        send(name, slot(src), slot(dst), target)

    quarter(far, 1 - z_lo)
    pl.semaphore_wait(barrier, len(peers))
    send("v", far, slot(V), near_z)
    quarter(slot(A), z_lo)
    move("a+", A, A_DOWN, up)
    move("a-", A, A_UP, down)

    loads[2].wait()
    loads[3].wait()
    for half in range(2):

        @pl.loop(0, TILE // UNIT)
        def _(i):
            at = pl.ds(pl.multiple_of(half * TILE + i * UNIT, UNIT), UNIT)
            own[0, at, :width] = normalize(full_s[at], width)[1].astype(jnp.bfloat16)
            own[0, at, width:] = -(normalize(full_t[at], width)[1].astype(jnp.bfloat16))
            total[0, at] = jnp.zeros((UNIT, width), jnp.float32)
            total[1, at] = jnp.zeros((UNIT, width), jnp.float32)

        at = pl.ds(half * TILE, TILE)
        send(f"k{half}", own.at[0, at], own.at[1, at], sibling)

    def relate(partner, start, block, tile):
        at, tokens = pl.ds(tile * TILE, TILE), pl.ds(start, GROUP)
        delta = lax.dot_general(
            own[block, at, :], partner[tokens, :], (((1,), (1,)), ((), ())),
            preferred_element_type=jnp.float32,
        )
        shrink = jnp.maximum(delta - margin, 0.0) + jnp.minimum(delta + margin, 0.0)
        relation = (weight * shrink).astype(jnp.bfloat16)
        for first, size in PARTS:
            total[block, at, pl.ds(first, size)] += jnp.dot(
                relation, partner[tokens, pl.ds(first, size)], preferred_element_type=jnp.float32
            )

    def relate_all(group):
        @pl.loop(0, 2)
        def _(block):
            for tile in range(rows // TILE):
                relate(cols, group * GROUP, block, tile)

    def relate_own(partner, start):
        for tile in range(rows // TILE):
            relate(partner, start, 0, tile)

    def share(name, start, size):
        send(name, cols.at[pl.ds(4 * GROUP + start, size)], extra.at[pl.ds(start, size)], sibling)

    arrived("v")
    move("v+", V, V_DOWN, up)
    move("v-", V, V_UP, down)
    move("w", V, W, after_z)
    arrived("a+", "a-")
    move("qd", A_DOWN, Q_DOWN, near_z)
    move("af", A_DOWN, A_FAR, up)
    move("qu", A_UP, Q_UP, near_z)
    move("q", A, Q, near_z)
    arrived("k0", "k1")
    relate_all(0)
    arrived("v+", "v-")
    move("vf", V_UP, V_FAR, down)
    arrived("w")
    move("w+", W, W_DOWN, up)
    move("w-", W, W_UP, down)
    relate_all(1)
    arrived("qd")
    move("qf", Q_DOWN, Q_FAR, up)
    arrived("af", "vf")
    relate_all(2)
    arrived("w-")
    move("wf", W_UP, W_FAR, down)
    arrived("w+", "qu")
    share("e", 0, 16)
    for tile in range(2):
        at = pl.ds(tile * TILE, TILE)
        relate(cols, 3 * GROUP, 1, tile)
        send(f"x{tile}", total.at[1, at], other.at[at], sibling)
    relate_own(cols, 3 * GROUP)
    place = pl.multiple_of(((bits[0] * 2 + bits[1]) * 2 + bits[2]) * UNIT, UNIT)
    scale, unit = normalize(full_s[pl.ds(place, UNIT)], width)
    own_unit[...] = unit
    own_scale[...] = jnp.broadcast_to(scale, own_scale.shape)
    for i, name in enumerate(("qf", "wf", "q")):
        arrived(name)
        share(f"e{name}", 16 + i * UNIT, UNIT)
    relate_own(cols, 4 * GROUP)
    arrived("x0", "x1", "e", "eqf", "ewf", "eq")
    relate_own(extra, 0)

    def chunk(wave, order, *place):
        strides = (4, 2, 1)
        index = sum(strides[d] * i for d, i in zip(order, place))
        skip, size = WAVES[wave]
        return pl.ds(pl.multiple_of(index * UNIT + skip, 16), size)

    def parts(wave):
        for part, (start, size) in enumerate(PARTS):
            order = ORDERS[(part + wave) % 3]
            yield part, order, [bits[d] for d in order], pl.ds(start, size)

    def reduce(step, wave, part, order, first, count):
        at = (pl.ds(first, count), pl.ds(*WAVES[wave]))
        send(f"r{part}{step}{wave}", rs_send[part].at[at], rs_recv[part].at[at], cube[order[step]])

    def spread(step, wave, part, order, *place):
        there = gathered[part].at[place + (slice(None),) * step + (pl.ds(*WAVES[wave]),)]
        send(f"g{part}{step}{wave}", there, there, cube[order[2 - step]])

    def halve_first(wave):
        sub = pl.ds(*WAVES[wave])
        for part, order, b, at in parts(wave):
            for i in range(4):
                rows_at = chunk(wave, order, 1 - b[0], i // 2, i % 2)
                rs_send[part][i, sub] = (total[0, rows_at, at] + other[rows_at, at]).astype(jnp.bfloat16)
            reduce(0, wave, part, order, 0, 4)

    def halve_second(wave):
        sub = pl.ds(*WAVES[wave])
        for part, order, b, at in parts(wave):
            arrived(f"r{part}0{wave}")
            for i in range(2):
                rows_at = chunk(wave, order, b[0], 1 - b[1], i)
                got = rs_recv[part][2 * (1 - b[1]) + i, sub].astype(jnp.float32)
                rs_send[part][4 + i, sub] = (
                    total[0, rows_at, at] + other[rows_at, at] + got
                ).astype(jnp.bfloat16)
            reduce(1, wave, part, order, 4, 2)

    def halve_third(wave):
        sub = pl.ds(*WAVES[wave])
        for part, order, b, at in parts(wave):
            arrived(f"r{part}1{wave}")
            for i, place in enumerate((1 - b[2], b[2])):
                rows_at = chunk(wave, order, b[0], b[1], place)
                value = (
                    total[0, rows_at, at] + other[rows_at, at]
                    + rs_recv[part][2 * b[1] + place, sub].astype(jnp.float32)
                    + rs_recv[part][4 + place, sub].astype(jnp.float32)
                )
                if i == 0:
                    rs_send[part][6, sub] = value.astype(jnp.bfloat16)
                    reduce(2, wave, part, order, 6, 1)
                else:
                    acc[sub, at] = value

    def finish(wave):
        sub = pl.ds(*WAVES[wave])
        for part, order, b, at in parts(wave):
            arrived(f"r{part}2{wave}")
            acc[sub, at] += rs_recv[part][6, sub].astype(jnp.float32)
        scale, unit = own_scale[sub, :1], own_unit[sub]
        unit_grad = acc[sub]
        dotted = jnp.sum(unit * unit_grad, axis=1, keepdims=True)
        grad = (scale * (unit_grad - unit * dotted)).astype(jnp.bfloat16)
        for part, order, b, at in parts(wave):
            start, size = PARTS[part]
            gathered[part][b[0], b[1], b[2], sub] = grad[:, start:start + size]
            spread(0, wave, part, order, *b)

    def double_second(wave):
        for part, order, b, at in parts(wave):
            arrived(f"g{part}0{wave}")
            spread(1, wave, part, order, b[0], b[1])

    def double_third(wave):
        for part, order, b, at in parts(wave):
            arrived(f"g{part}1{wave}")
            spread(2, wave, part, order, b[0])

    def emit(wave):
        sub = pl.ds(*WAVES[wave])
        for part, order, b, at in parts(wave):
            arrived(f"g{part}2{wave}")
            for i in range(8):
                place = (i // 4, i // 2 % 2, i % 2)
                out[chunk(wave, (0, 1, 2), *place), at] = gathered[part][
                    tuple(place[d] for d in order) + (sub,)
                ].astype(jnp.float32)

    stages = (halve_first, halve_second, halve_third, finish, double_second, double_third, emit)
    steps = [(wave + APART * i, i, wave) for i in range(len(stages)) for wave in range(len(WAVES))]
    for _, i, wave in sorted(steps):
        stages[i](wave)
    for name in NAMES:
        started[name].wait_send()


def local(student, teacher):
    rows, width = student.shape
    bf16, f32 = jnp.bfloat16, jnp.float32

    def body(student, teacher, out, *scratch):
        plain, parts = scratch[:10], scratch[10:19]
        kernel(student, teacher, out, *plain, parts[0:3], parts[3:6], parts[6:9], *scratch[19:])

    grad = pl.pallas_call(
        body,
        out_shape=pltpu.VMEM((rows, width), f32),
        in_specs=[pl.BlockSpec(memory_space=pl.ANY)] * 2,
        out_specs=pl.BlockSpec(memory_space=pltpu.VMEM),
        scratch_shapes=[
            pltpu.VMEM((2 * UNIT, width), f32),
            pltpu.VMEM((2 * UNIT, width), f32),
            pltpu.VMEM((rows, width), f32),
            pltpu.VMEM((rows, width), f32),
            pltpu.VMEM((UNIT, 2 * width), bf16),
            pltpu.VMEM((2 * rows, 2 * width), bf16),
            pltpu.VMEM((GROUP, 2 * width), bf16),
            pltpu.VMEM((2, rows, 2 * width), bf16),
            pltpu.VMEM((2, rows, width), f32),
            pltpu.VMEM((rows, width), f32),
        ]
        + [pltpu.VMEM((7, UNIT, size), bf16) for _, size in PARTS] * 2
        + [pltpu.VMEM((2, 2, 2, UNIT, size), bf16) for _, size in PARTS]
        + [
            pltpu.VMEM((UNIT, width), f32),
            pltpu.VMEM((UNIT, width), f32),
            pltpu.VMEM((UNIT, 128), f32),
            pltpu.SemaphoreType.DMA((4,)),
            pltpu.SemaphoreType.DMA((len(NAMES),)),
            pltpu.SemaphoreType.DMA((len(NAMES),)),
        ],
        compiler_params=pltpu.CompilerParams(
            collective_id=0, has_side_effects=True, vmem_limit_bytes=56 << 20
        ),
        name="relation_grad",
    )(student, teacher)
    return grad


def solution(mesh):
    placed = (P("seq", None), P("seq", None))
    return jax.shard_map(
        local, mesh=mesh, in_specs=placed, out_specs=P("seq", None), check_vma=False
    )
```

```python
import functools
import math

import jax
import jax.numpy as jnp
from jax import lax
from jax.experimental import pallas as pl
from jax.experimental.pallas import tpu as pltpu
from jax.sharding import PartitionSpec as P

MESH = pl.DeviceIdType.MESH
UNIT = 80
GROUP = 256
TILE = 320
WAVES = ((0, 32), (32, 32), (64, 16))
APART = 2
PARTS = ((0, 512), (512, 512), (1024, 384))
ORDERS = ((0, 1, 2), (1, 2, 0), (2, 0, 1))

NAMES = (
    ["v", "q", "w", "qd", "qu", "qf", "a+", "a-", "af", "v+", "v-", "vf", "w+", "w-", "wf"]
    + ["e", "eqf", "ewf", "eq", "k0", "k1", "x0", "x1"]
    + [f"{kind}{part}{step}{wave}" for kind in "rg"
       for part in range(3) for step in range(3) for wave in range(len(WAVES))]
)
INDEX = {name: i for i, name in enumerate(NAMES)}


def normalize(values, width):
    scale = lax.rsqrt(jnp.sum(values * values, axis=1, keepdims=True) + width * 1e-06)
    return scale, values * scale


def kernel(
    student, teacher, out,
    quarter_s, quarter_t, full_s, full_t, far, cols, extra, own, total, other,
    rs_send, rs_recv, gathered, acc, own_unit, own_scale, load_sem, send_sem, recv_sem,
):
    rows, width = student.shape
    margin = 0.75 / math.sqrt(width)
    weight = 64.0 * width / math.sqrt(rows * lax.axis_size("seq"))

    seq, pair = lax.axis_index("seq"), lax.axis_index("pair")
    core, y, z_hi = seq % 2, (seq // 2) % 4, seq // 8
    z_lo, x = pair // 4, pair % 4
    z = z_hi * 2 + z_lo
    side = 2 * z_lo - 1

    def device(x=x, y=y, z=z, core=core):
        return ((z // 2 * 4 + y) * 2 + core, (z % 2) * 4 + x)

    up, down = device(y=(y + 1) % 4), device(y=(y + 3) % 4)
    near_z = device(z=(z + side + 8) % 8)
    after_z, before_z = device(z=(z - 2 * side + 8) % 8), device(z=(z + 2 * side + 8) % 8)
    sibling = device(core=1 - core)
    cube = (device(x=x + 1 - 2 * (x % 2)), device(x=3 - x), device(z=z + 1 - 2 * z_lo))
    bits = (((x + 1) // 2) % 2, x // 2, z_lo)

    def copy(name, src, dst, target):
        i = INDEX[name]
        return pltpu.make_async_remote_copy(
            src_ref=src, dst_ref=dst, send_sem=send_sem.at[i], recv_sem=recv_sem.at[i],
            device_id=target, device_id_type=MESH,
        )

    started = {}

    def send(name, src, dst, target):
        started[name] = copy(name, src, dst, target)
        started[name].start()

    def arrived(*names):
        for name in names:
            started[name].wait_recv()

    barrier = pltpu.get_barrier_semaphore()
    peers = (up, down, near_z, after_z, before_z, sibling) + cube
    for peer in peers:
        pl.semaphore_signal(barrier, inc=1, device_id=peer, device_id_type=MESH)

    first = pl.multiple_of(x * (2 * UNIT), 2 * UNIT)
    loads = [
        pltpu.make_async_copy(student.at[pl.ds(first, 2 * UNIT)], quarter_s, load_sem.at[0]),
        pltpu.make_async_copy(teacher.at[pl.ds(first, 2 * UNIT)], quarter_t, load_sem.at[1]),
        pltpu.make_async_copy(student, full_s, load_sem.at[2]),
        pltpu.make_async_copy(teacher, full_t, load_sem.at[3]),
    ]
    loads[0].start()
    loads[1].start()

    (A, A_DOWN, A_UP, V, V_DOWN, V_UP, W, A_FAR, V_FAR, Q_DOWN,
     W_DOWN, W_UP, Q_UP, Q_FAR, W_FAR, Q) = range(16)

    loads[0].wait()
    loads[1].wait()
    loads[2].start()
    loads[3].start()
    def quarter(dst, start):
        at = pl.ds(pl.multiple_of(start * UNIT, UNIT), UNIT)
        dst[:, :width] = normalize(quarter_s[at], width)[1].astype(jnp.bfloat16)
        dst[:, width:] = normalize(quarter_t[at], width)[1].astype(jnp.bfloat16)

    def slot(i):
        return cols.at[pl.ds(i * UNIT, UNIT)]

    def move(name, src, dst, target):
        send(name, slot(src), slot(dst), target)

    quarter(far, 1 - z_lo)
    pl.semaphore_wait(barrier, len(peers))
    send("v", far, slot(V), near_z)
    quarter(slot(A), z_lo)
    move("a+", A, A_DOWN, up)
    move("a-", A, A_UP, down)

    loads[2].wait()
    loads[3].wait()
    for half in range(2):

        @pl.loop(0, TILE // UNIT)
        def _(i):
            at = pl.ds(pl.multiple_of(half * TILE + i * UNIT, UNIT), UNIT)
            own[0, at, :width] = normalize(full_s[at], width)[1].astype(jnp.bfloat16)
            own[0, at, width:] = -(normalize(full_t[at], width)[1].astype(jnp.bfloat16))
            total[0, at] = jnp.zeros((UNIT, width), jnp.float32)
            total[1, at] = jnp.zeros((UNIT, width), jnp.float32)

        at = pl.ds(half * TILE, TILE)
        send(f"k{half}", own.at[0, at], own.at[1, at], sibling)

    def relate(partner, start, block, tile, size=TILE):
        at, tokens = pl.ds(tile * size, size), pl.ds(start, GROUP)
        delta = lax.dot_general(
            own[block, at, :], partner[tokens, :], (((1,), (1,)), ((), ())),
            preferred_element_type=jnp.float32,
        )
        shrink = jnp.maximum(delta - margin, 0.0) + jnp.minimum(delta + margin, 0.0)
        relation = (weight * shrink).astype(jnp.bfloat16)
        for first, wide in PARTS:
            total[block, at, pl.ds(first, wide)] += jnp.dot(
                relation, partner[tokens, pl.ds(first, wide)], preferred_element_type=jnp.float32
            )

    def relate_all(group):
        @pl.loop(0, 2)
        def _(block):
            for tile in range(rows // TILE):
                relate(cols, group * GROUP, block, tile)

    def relate_own(partner, start):
        relate(partner, start, 0, 0, rows)

    def share(name, start, size):
        send(name, cols.at[pl.ds(4 * GROUP + start, size)], extra.at[pl.ds(start, size)], sibling)

    arrived("v")
    move("v+", V, V_DOWN, up)
    move("v-", V, V_UP, down)
    move("w", V, W, after_z)
    arrived("a+", "a-")
    move("qd", A_DOWN, Q_DOWN, near_z)
    move("af", A_DOWN, A_FAR, up)
    move("qu", A_UP, Q_UP, near_z)
    move("q", A, Q, near_z)
    arrived("k0", "k1")
    relate_all(0)
    arrived("v+", "v-")
    move("vf", V_UP, V_FAR, down)
    arrived("w")
    move("w+", W, W_DOWN, up)
    move("w-", W, W_UP, down)
    relate_all(1)
    arrived("qd")
    move("qf", Q_DOWN, Q_FAR, up)
    arrived("af", "vf")
    relate_all(2)
    arrived("w-")
    move("wf", W_UP, W_FAR, down)
    arrived("w+", "qu")
    share("e", 0, 16)
    for tile in range(2):
        at = pl.ds(tile * TILE, TILE)
        relate(cols, 3 * GROUP, 1, tile)
        send(f"x{tile}", total.at[1, at], other.at[at], sibling)
    relate_own(cols, 3 * GROUP)
    place = pl.multiple_of(((bits[0] * 2 + bits[1]) * 2 + bits[2]) * UNIT, UNIT)
    scale, unit = normalize(full_s[pl.ds(place, UNIT)], width)
    own_unit[...] = unit
    own_scale[...] = jnp.broadcast_to(scale, own_scale.shape)
    for i, name in enumerate(("qf", "wf", "q")):
        arrived(name)
        share(f"e{name}", 16 + i * UNIT, UNIT)
    relate_own(cols, 4 * GROUP)
    arrived("x0", "x1", "e", "eqf", "ewf", "eq")
    relate_own(extra, 0)

    def chunk(wave, order, *place):
        strides = (4, 2, 1)
        index = sum(strides[d] * i for d, i in zip(order, place))
        skip, size = WAVES[wave]
        return pl.ds(pl.multiple_of(index * UNIT + skip, 16), size)

    def parts(wave):
        for part, (start, size) in enumerate(PARTS):
            order = ORDERS[(part + wave) % 3]
            yield part, order, [bits[d] for d in order], pl.ds(start, size)

    def reduce(step, wave, part, order, first, count):
        at = (pl.ds(first, count), pl.ds(*WAVES[wave]))
        send(f"r{part}{step}{wave}", rs_send[part].at[at], rs_recv[part].at[at], cube[order[step]])

    def spread(step, wave, part, order, *place):
        there = gathered[part].at[place + (slice(None),) * step + (pl.ds(*WAVES[wave]),)]
        send(f"g{part}{step}{wave}", there, there, cube[order[2 - step]])

    def halve_first(wave):
        sub = pl.ds(*WAVES[wave])
        for part, order, b, at in parts(wave):
            for i in range(4):
                rows_at = chunk(wave, order, 1 - b[0], i // 2, i % 2)
                rs_send[part][i, sub] = (total[0, rows_at, at] + other[rows_at, at]).astype(jnp.bfloat16)
            reduce(0, wave, part, order, 0, 4)

    def halve_second(wave):
        sub = pl.ds(*WAVES[wave])
        for part, order, b, at in parts(wave):
            arrived(f"r{part}0{wave}")
            for i in range(2):
                rows_at = chunk(wave, order, b[0], 1 - b[1], i)
                got = rs_recv[part][2 * (1 - b[1]) + i, sub].astype(jnp.float32)
                rs_send[part][4 + i, sub] = (
                    total[0, rows_at, at] + other[rows_at, at] + got
                ).astype(jnp.bfloat16)
            reduce(1, wave, part, order, 4, 2)

    def halve_third(wave):
        sub = pl.ds(*WAVES[wave])
        for part, order, b, at in parts(wave):
            arrived(f"r{part}1{wave}")
            for i, place in enumerate((1 - b[2], b[2])):
                rows_at = chunk(wave, order, b[0], b[1], place)
                value = (
                    total[0, rows_at, at] + other[rows_at, at]
                    + rs_recv[part][2 * b[1] + place, sub].astype(jnp.float32)
                    + rs_recv[part][4 + place, sub].astype(jnp.float32)
                )
                if i == 0:
                    rs_send[part][6, sub] = value.astype(jnp.bfloat16)
                    reduce(2, wave, part, order, 6, 1)
                else:
                    acc[sub, at] = value

    def finish(wave):
        sub = pl.ds(*WAVES[wave])
        for part, order, b, at in parts(wave):
            arrived(f"r{part}2{wave}")
            acc[sub, at] += rs_recv[part][6, sub].astype(jnp.float32)
        scale, unit = own_scale[sub, :1], own_unit[sub]
        unit_grad = acc[sub]
        dotted = jnp.sum(unit * unit_grad, axis=1, keepdims=True)
        grad = (scale * (unit_grad - unit * dotted)).astype(jnp.bfloat16)
        for part, order, b, at in parts(wave):
            start, size = PARTS[part]
            gathered[part][b[0], b[1], b[2], sub] = grad[:, start:start + size]
            spread(0, wave, part, order, *b)

    def double_second(wave):
        for part, order, b, at in parts(wave):
            arrived(f"g{part}0{wave}")
            spread(1, wave, part, order, b[0], b[1])

    def double_third(wave):
        for part, order, b, at in parts(wave):
            arrived(f"g{part}1{wave}")
            spread(2, wave, part, order, b[0])

    def emit(wave):
        sub = pl.ds(*WAVES[wave])
        for part, order, b, at in parts(wave):
            arrived(f"g{part}2{wave}")
            for i in range(8):
                place = (i // 4, i // 2 % 2, i % 2)
                out[chunk(wave, (0, 1, 2), *place), at] = gathered[part][
                    tuple(place[d] for d in order) + (sub,)
                ].astype(jnp.float32)

    stages = (halve_first, halve_second, halve_third, finish, double_second, double_third, emit)
    steps = [(wave + APART * i, i, wave) for i in range(len(stages)) for wave in range(len(WAVES))]
    settled = set()

    def settle(kinds):
        for name in started:
            if name[0] in kinds and name not in settled:
                settled.add(name)
                started[name].wait_send()

    for _, i, wave in sorted(steps):
        if (i, wave) == (1, 0):
            settle("vqawekx")
        elif (i, wave) == (6, 0):
            settle("r")
        stages[i](wave)
    settle("g")


def local(student, teacher):
    rows, width = student.shape
    bf16, f32 = jnp.bfloat16, jnp.float32

    def body(student, teacher, out, *scratch):
        plain, parts = scratch[:10], scratch[10:19]
        kernel(student, teacher, out, *plain, parts[0:3], parts[3:6], parts[6:9], *scratch[19:])

    grad = pl.pallas_call(
        body,
        out_shape=pltpu.VMEM((rows, width), f32),
        in_specs=[pl.BlockSpec(memory_space=pl.ANY)] * 2,
        out_specs=pl.BlockSpec(memory_space=pltpu.VMEM),
        scratch_shapes=[
            pltpu.VMEM((2 * UNIT, width), f32),
            pltpu.VMEM((2 * UNIT, width), f32),
            pltpu.VMEM((rows, width), f32),
            pltpu.VMEM((rows, width), f32),
            pltpu.VMEM((UNIT, 2 * width), bf16),
            pltpu.VMEM((2 * rows, 2 * width), bf16),
            pltpu.VMEM((GROUP, 2 * width), bf16),
            pltpu.VMEM((2, rows, 2 * width), bf16),
            pltpu.VMEM((2, rows, width), f32),
            pltpu.VMEM((rows, width), f32),
        ]
        + [pltpu.VMEM((7, UNIT, size), bf16) for _, size in PARTS] * 2
        + [pltpu.VMEM((2, 2, 2, UNIT, size), bf16) for _, size in PARTS]
        + [
            pltpu.VMEM((UNIT, width), f32),
            pltpu.VMEM((UNIT, width), f32),
            pltpu.VMEM((UNIT, 128), f32),
            pltpu.SemaphoreType.DMA((4,)),
            pltpu.SemaphoreType.DMA((len(NAMES),)),
            pltpu.SemaphoreType.DMA((len(NAMES),)),
        ],
        compiler_params=pltpu.CompilerParams(
            collective_id=0, has_side_effects=True, vmem_limit_bytes=56 << 20
        ),
        name="relation_grad",
    )(student, teacher)
    return grad


def solution(mesh):
    placed = (P("seq", None), P("seq", None))
    return jax.shard_map(
        local, mesh=mesh, in_specs=placed, out_specs=P("seq", None), check_vma=False
    )
```
